32 devices in a mesh: dp: 8 (over z, y), tensor: 4 (over x, core).
Axes of the slice: x: 2, y: 2, z: 4, core: 2. Of those that a mesh axis runs over, the one named last changes fastest.
Arguments:
- tokens: bfloat16 [16384, 1024], P('dp', 'tensor'), may hold values from -6 to 6
- lengths: int32 [8, 6], P('dp'), may hold values from 0 to 1024, as said below
- gain_one: bfloat16 [1024], P('tensor'), may hold values from 0.5 to 1.5
- weight_in: bfloat16 [3, 1024, 1024], P(None, None, 'tensor'), may hold values from -0.1875 to 0.1875
- conv_taps: bfloat16 [3, 1024], P(None, 'tensor'), may hold values from -1 to 1
- weight_out: bfloat16 [1024, 1024], P('tensor'), may hold values from -0.1875 to 0.1875
- gain_two: bfloat16 [1024], P('tensor'), may hold values from 0.5 to 1.5
- weight_feed: bfloat16 [2, 1024, 4608], P(None, None, 'tensor'), may hold values from -0.1875 to 0.1875
- weight_down: bfloat16 [4608, 1024], P('tensor'), may hold values from -0.09375 to 0.09375
- grad_out: bfloat16 [16384, 1024], P('dp', 'tensor'), may hold values from -6 to 6
Outputs:
- block_out: bfloat16 [16384, 1024], P('dp', 'tensor')
- grad_tokens: bfloat16 [16384, 1024], P('dp', 'tensor')
- grad_gain_one: float32 [1024], P('tensor')
- grad_weight_in: float32 [3, 1024, 1024], P(None, 'dp', 'tensor')
- grad_conv_taps: float32 [3, 1024], P(None, 'tensor')
- grad_weight_out: float32 [1024, 1024], P('tensor', 'dp')
- grad_gain_two: float32 [1024], P('tensor')
- grad_weight_feed: float32 [2, 1024, 4608], P(None, 'dp', 'tensor')
- grad_weight_down: float32 [4608, 1024], P('tensor', 'dp')
The draws below stay inside these ranges and needn't reach their ends.
Inputs may be any that keep to these rules, and one draw needn't show every extreme that they name: `lengths`: row g lists the documents of the slots of index g of dp in order, zeros being empty slots; each row sums to at most 2048, some row to exactly 2048, and some document has exactly 1024 tokens.
All inputs are finite; a program needn't handle non-finite values.
Results may differ from the reference program's by a relative error of at most 0.0091.
Values may be sent and summed in bfloat16 or wider, within the bound.
A program may use at most 192 MiB of HBM per device.

```python
import jax
import jax.numpy as jnp
from jax import lax

D = 1024
FF = 4608
TAPS = 3
MAXLEN = 1024
TOK_DEV = 2048
SEQS = 6
TOKENS = 16384
N_DP = 8


def draw_lengths(key, part):
    key = jax.random.fold_in(key, 11)
    keys = jax.random.split(key, 5)
    raw_lens = jax.random.randint(keys[0], (N_DP, SEQS), 1, MAXLEN + 1)
    full_lens = jax.random.randint(keys[1], (N_DP, SEQS), TOK_DEV // SEQS + 1, MAXLEN + 1)
    full_device = jax.random.randint(keys[2], (), 0, N_DP)
    is_full = jnp.arange(N_DP) == full_device
    raw_lens = jnp.where(is_full[:, None], full_lens, raw_lens)
    forced = (jax.random.randint(keys[3], (N_DP,), 0, 2) == 1) | is_full
    first_lens = jnp.where(forced, MAXLEN, raw_lens[:, 0])
    raw_lens = jnp.concatenate([first_lens[:, None], raw_lens[:, 1:]], axis=1)
    target = jax.random.randint(keys[4], (N_DP,), TOK_DEV // 2, TOK_DEV + 1)
    target = jnp.where(is_full, TOK_DEV, target)
    doc_ends = jnp.cumsum(raw_lens, axis=1)
    doc_starts = doc_ends - raw_lens
    result = jnp.clip(target[:, None] - doc_starts, 0, raw_lens)
    return result.astype(jnp.int32)


def with_spikes(drawn, rng, source, target, blocks, factor):
    def block_of(dim):
        return (jnp.arange(drawn.shape[dim]) // (drawn.shape[dim] // blocks)).reshape((-1,) + (1,) * (drawn.ndim - 1 - dim))

    first = jax.random.permutation(rng, blocks)[block_of(target)]
    second = (block_of(target) + blocks // 2) % blocks
    return jnp.where((block_of(source) == first) | (block_of(source) == second), factor * drawn, drawn)


def steps_of(own_key, extent, cuts, smallest, high):
    factor_of = 1.0
    for axis_at, shards_of in cuts:
        draws = jax.random.uniform(jax.random.fold_in(jax.random.fold_in(own_key, 6), axis_at), (shards_of,), jnp.float32, smallest / len(cuts), high / len(cuts))
        factor_of = factor_of * jnp.repeat(jnp.exp(draws), extent[axis_at] // shards_of).reshape((-1,) + (1,) * (len(extent) - 1 - axis_at))
    return factor_of


def scatter_about(key, shape, width, limit, cuts=(), kind=jnp.bfloat16):
    values = jax.random.normal(key, shape, jnp.float32) * width
    if len(cuts) > 0:
        values = steps_of(key, shape, cuts, -0.22, 0.18) * values
    return jnp.clip(values, min=-limit, max=limit).astype(kind)


def noise_with(key, extent, deviation, bound, pieces, heavy, kind=jnp.bfloat16):
    drawn = deviation * jax.random.normal(key, extent, jnp.float32)
    if pieces:
        drawn = drawn * steps_of(key, extent, pieces, -0.22, 0.18)
    return jnp.clip(with_spikes(drawn, jax.random.fold_in(key, 3), *heavy), -bound, bound).astype(kind)


def setup_inputs(seed: int = 0) -> dict:
    seeds = jax.random.split(jax.random.key(seed), 11)
    return {
        "tokens": scatter_about(seeds[0], (TOKENS, D), 1.0, 6.0, ((0, 8), (1, 4))),
        "lengths": draw_lengths(jax.random.fold_in(seeds[10], 71), 0),
        "gain_one": jnp.clip(1.0 + 0.1 * jax.random.normal(seeds[2], (D,), jnp.float32), 0.5, 1.5).astype(jnp.bfloat16),
        "weight_in": scatter_about(seeds[3], (3, D, D), D ** -0.5, 0.1875, ((2, 4),)),
        "conv_taps": jnp.clip(jax.random.uniform(seeds[4], (TAPS, D), jnp.float32, -1.0, 1.0) * steps_of(seeds[4], (TAPS, D), ((1, 4),), -0.4, 0.0), -1.0, 1.0).astype(jnp.bfloat16),
        "weight_out": scatter_about(seeds[5], (D, D), D ** -0.5, 0.1875, ((0, 4),)),
        "gain_two": jnp.clip(1.0 + 0.1 * jax.random.normal(seeds[6], (D,), jnp.float32), 0.5, 1.5).astype(jnp.bfloat16),
        "weight_feed": scatter_about(seeds[7], (2, D, FF), D ** -0.5, 0.1875, ((2, 4),)),
        "weight_down": scatter_about(seeds[8], (FF, D), FF ** -0.5, 0.09375, ((0, 4),)),
        "grad_out": noise_with(seeds[9], (TOKENS, D), 1.0, 6.0, ((0, 8), (1, 4)), (0, 1, 8, 2.0)),
    }


@jax.custom_vjp
def low(v):
    return lax.optimization_barrier(v.astype(jnp.bfloat16)).astype(jnp.float32)

@jax.custom_vjp
def low_back(v):
    return v

def low_keep(v):
    return (low(v), None)

def low_pass(kept, grad):
    return (grad,)

def back_keep(v):
    return (v, None)

def back_low(kept, grad):
    return (low(grad),)
low.defvjp(low_keep, low_pass)
low_back.defvjp(back_keep, back_low)
EPSILON = 1e-05
PRECISE = lax.Precision.HIGHEST

def row_masks(doc_lens, row_count):
    doc_ends = jnp.cumsum(doc_lens)
    positions = jnp.arange(row_count, dtype=jnp.int32)
    segments = lax.optimization_barrier(jnp.sum((positions[:, None] >= doc_ends[None, :]).astype(jnp.int32), axis=1))
    live_mask = (positions < doc_ends[-1]).astype(jnp.float32)[:, None]
    same_one = jnp.concatenate([jnp.zeros((1,), jnp.float32), (segments[1:] == segments[:-1]).astype(jnp.float32)])
    same_two = jnp.concatenate([jnp.zeros((2,), jnp.float32), (segments[2:] == segments[:-2]).astype(jnp.float32)])
    return (live_mask, same_one[:, None], same_two[:, None])

def shift_down(values, offset):
    return jnp.concatenate([jnp.zeros((offset,) + values.shape[1:], values.dtype), values[:-offset]], axis=0)

def block_forward(tokens_in, gain_one, weight_in, conv_taps, weight_out, gain_two, weight_feed, weight_down, live_mask, same_one, same_two):
    scale_one = lax.rsqrt(lax.optimization_barrier(jnp.mean(tokens_in * tokens_in, axis=1, keepdims=True)) + EPSILON)
    normed_one = low(tokens_in * scale_one * gain_one)
    gate_block = low_back(jnp.einsum('td,gde->gte', normed_one, weight_in, precision=PRECISE))
    mixed_in = gate_block[0] * gate_block[2]
    prev_one = shift_down(mixed_in, 1) * same_one
    prev_two = shift_down(mixed_in, 2) * same_two
    conv_out = conv_taps[2] * mixed_in + conv_taps[1] * prev_one + conv_taps[0] * prev_two
    mixer_rows = low(gate_block[1] * conv_out)
    mixer_out = low_back(jnp.dot(mixer_rows, weight_out, precision=PRECISE))
    middle = tokens_in + live_mask * mixer_out
    scale_two = lax.rsqrt(lax.optimization_barrier(jnp.mean(middle * middle, axis=1, keepdims=True)) + EPSILON)
    normed_two = low(middle * scale_two * gain_two)
    gate_up = low_back(jnp.einsum('td,kdf->ktf', normed_two, weight_feed, precision=PRECISE))
    hidden = low(jax.nn.silu(gate_up[0]) * gate_up[1])
    feed_out = low_back(jnp.dot(hidden, weight_down, precision=PRECISE))
    return middle + live_mask * feed_out

def reference(tokens, lengths, gain_one, weight_in, conv_taps, weight_out, gain_two, weight_feed, weight_down, grad_out):
    weights = tuple((array_item.astype(jnp.float32) for array_item in (gain_one, weight_in, conv_taps, weight_out, gain_two, weight_feed, weight_down)))
    token_blocks = tokens.astype(jnp.float32).reshape(N_DP, TOK_DEV, D)
    grad_blocks = grad_out.astype(jnp.float32).reshape(N_DP, TOK_DEV, D)

    def device_step(grad_totals, inputs_tuple):
        token_rows, grad_rows, doc_lens = inputs_tuple
        live_mask, same_one, same_two = row_masks(doc_lens, TOK_DEV)

        def forward(token_arg, *weight_args):
            return block_forward(token_arg, *weight_args, live_mask, same_one, same_two)
        result, pullback = jax.vjp(forward, token_rows, *weights)
        cotangents = pullback(grad_rows)
        grad_totals = tuple((total_item + grad_item for total_item, grad_item in zip(grad_totals, cotangents[1:])))
        return (grad_totals, (result.astype(jnp.bfloat16), cotangents[0].astype(jnp.bfloat16)))
    zero_grads = tuple((jnp.zeros_like(array_item) for array_item in weights))
    grad_totals, (result_rows, input_grads) = lax.scan(device_step, zero_grads, (token_blocks, grad_blocks, lengths))
    return (result_rows.reshape(TOKENS, D), input_grads.reshape(TOKENS, D), grad_totals[0], grad_totals[1], grad_totals[2], grad_totals[3], grad_totals[4], grad_totals[5], grad_totals[6])
```

```python
import jax
import jax.numpy as jnp
from jax import lax
from jax.sharding import PartitionSpec as P

EPSILON = 1e-05
CHUNKS = 2
F32 = jnp.float32
BF16 = jnp.bfloat16


def swap_core(values):
    size = lax.axis_size("tensor")
    return lax.ppermute(values, "tensor", [(i, i ^ 1) for i in range(size)])


def swap_chip(values):
    size = lax.axis_size("tensor")
    return lax.ppermute(values, "tensor", [(i, i ^ 2) for i in range(size)])


def ordered(is_first, own, other):
    return jnp.where(
        is_first,
        jnp.concatenate([own, other], axis=-1),
        jnp.concatenate([other, own], axis=-1),
    )


def gather_columns(values, core, chip):
    from_chip = swap_chip(values)
    from_core = swap_core(values)
    from_both = swap_core(from_chip)
    near = ordered(core == 0, values, from_core)
    far = ordered(core == 0, from_chip, from_both)
    return ordered(chip == 0, near, far)


def split_columns(weight, axis, core, chip):
    width = weight.shape[axis] // 4

    def block(chip_at, core_at):
        return lax.dynamic_slice_in_dim(weight, (chip_at * 2 + core_at) * width, width, axis)

    kept = jnp.concatenate([block(1 - chip, core), block(chip, core)], axis=axis)
    sent = jnp.concatenate([block(1 - chip, 1 - core), block(chip, 1 - core)], axis=axis)
    return sent, kept


def scatter_columns(sent, kept):
    total = kept + swap_core(sent.astype(BF16)).astype(F32)
    width = total.shape[1] // 2
    return total[:, width:] + swap_chip(total[:, :width].astype(BF16)).astype(F32)


def sum_tensor(values):
    values = values + swap_core(values)
    return values + swap_chip(values)


def sum_groups(values):
    size = lax.axis_size("dp")
    step = 1
    while step < size:
        values = values + lax.ppermute(values, "dp", [(i, i ^ step) for i in range(size)])
        step *= 2
    return values


def total_of(parts):
    result = parts[0]
    for part in parts[1:]:
        result = result + part
    return result


def dot_rows(left, right):
    return lax.dot_general(left, right, (((0,), (0,)), ((), ())), preferred_element_type=F32)


def dot_last(left, right):
    return lax.dot_general(left, right, (((1,), (1,)), ((), ())), preferred_element_type=F32)


def body(
    tokens,
    lengths,
    gain_one,
    weight_in,
    conv_taps,
    weight_out,
    gain_two,
    weight_feed,
    weight_down,
    grad_out,
):
    row_count = tokens.shape[0]
    part_width = tokens.shape[1]
    full_width = part_width * lax.axis_size("tensor")
    index = lax.axis_index("tensor")
    core, chip = index % 2, index // 2
    doc_ends = jnp.cumsum(lengths[0])
    positions = jnp.arange(row_count, dtype=jnp.int32)
    segments = jnp.sum((positions[:, None] >= doc_ends[None, :]).astype(jnp.int32), axis=1)
    live_all = (positions < doc_ends[-1]).astype(F32)[:, None]
    same_one_all = jnp.concatenate(
        [jnp.zeros((1,), F32), (segments[1:] == segments[:-1]).astype(F32)]
    )[:, None]
    same_two_all = jnp.concatenate(
        [jnp.zeros((2,), F32), (segments[2:] == segments[:-2]).astype(F32)]
    )[:, None]
    rows = row_count // CHUNKS

    def cut(array):
        return [array[k * rows : (k + 1) * rows] for k in range(CHUNKS)]

    live, same_one, same_two = cut(live_all), cut(same_one_all), cut(same_two_all)
    token_parts, grad_parts = cut(tokens), cut(grad_out)
    span = range(CHUNKS)

    gains = gather_columns(jnp.stack([gain_one, gain_two]), core, chip).astype(F32)
    gain_one_full, gain_two_full = gains[0:1], gains[1:2]
    token_full = [gather_columns(part, core, chip) for part in token_parts]
    held = lax.optimization_barrier(tuple(grad_parts) + tuple(token_full))
    grad_later, token_full = held[:CHUNKS], held[CHUNKS:]

    out_sent, out_kept = split_columns(weight_out, 1, core, chip)
    down_sent, down_kept = split_columns(weight_down, 1, core, chip)
    feed_sent, feed_kept = split_columns(weight_feed, 1, core, chip)
    in_sent, in_kept = split_columns(weight_in, 1, core, chip)
    taps = conv_taps.astype(F32)

    normed_one, gates, mixed, prev_one, prev_two, conv = [], [], [], [], [], []
    mixer_rows, middle, middle_full, scale_one = [], [], [], []
    for k in span:
        wide = token_full[k].astype(F32)
        scale = lax.rsqrt(jnp.mean(wide * wide, axis=1, keepdims=True) + EPSILON)
        scale_one.append(scale)
        normed_one.append((wide * scale * gain_one_full).astype(BF16))
        gate = jnp.einsum("td,gde->gte", normed_one[k], weight_in, preferred_element_type=F32)
        gates.append(gate)
        mix = gate[0] * gate[2]
        mixed.append(mix)
        before = mixed[k - 1][-2:] if k else jnp.zeros((2, part_width), F32)
        extended = jnp.concatenate([before, mix], axis=0)
        prev_one.append(extended[1:-1] * same_one[k])
        prev_two.append(extended[:-2] * same_two[k])
        conv.append(taps[2] * mix + taps[1] * prev_one[k] + taps[0] * prev_two[k])
        mixer_rows.append((gate[1] * conv[k]).astype(BF16))
        mixer_out = scatter_columns(
            jnp.dot(mixer_rows[k], out_sent, preferred_element_type=F32),
            jnp.dot(mixer_rows[k], out_kept, preferred_element_type=F32),
        )
        middle.append(token_parts[k].astype(F32) + live[k] * mixer_out)
        middle_full.append(gather_columns(middle[k].astype(BF16), core, chip))

    grad_full = [gather_columns(part, core, chip) for part in grad_later]
    normed_two, hidden, feed_grad, gu_grad, block_out = [], [], [], [], []
    middle_grad, mixer_grad, gain_two_parts = [], [], []
    for k in span:
        wide = middle_full[k].astype(F32)
        scale = lax.rsqrt(jnp.mean(wide * wide, axis=1, keepdims=True) + EPSILON)
        normed_two.append((wide * scale * gain_two_full).astype(BF16))
        gate_up = jnp.einsum("td,kdf->ktf", normed_two[k], weight_feed, preferred_element_type=F32)
        gate, up = gate_up[0], gate_up[1]
        sigmoid = jax.nn.sigmoid(gate)
        hidden.append((gate * sigmoid * up).astype(BF16))
        feed_grad.append(jnp.where(live[k] > 0.0, grad_full[k], jnp.zeros_like(grad_full[k])))
        hidden_grad = dot_last(feed_grad[k], weight_down)
        gate_grad = hidden_grad * up * sigmoid * (1.0 + gate * (1.0 - sigmoid))
        up_grad = hidden_grad * (gate * sigmoid)
        inner = sum_tensor(jnp.sum(gate_grad * gate + up_grad * up, axis=1))
        gu_grad.append(jnp.stack([gate_grad, up_grad]).astype(BF16))
        normed_grad = scatter_columns(
            jnp.einsum("ktf,kdf->td", gu_grad[k], feed_sent, preferred_element_type=F32),
            jnp.einsum("ktf,kdf->td", gu_grad[k], feed_kept, preferred_element_type=F32),
        )
        unit = middle[k] * scale
        gain_two_parts.append(jnp.sum(normed_grad * unit, axis=0))
        middle_grad.append(
            grad_parts[k].astype(F32)
            + scale
            * (normed_grad * gain_two.astype(F32) - unit * (inner / full_width)[:, None])
        )
        mixer_grad.append(gather_columns((middle_grad[k] * live[k]).astype(BF16), core, chip))
    grad_feed = total_of(
        [
            jnp.einsum("td,ktf->kdf", normed_two[k], gu_grad[k], preferred_element_type=F32)
            for k in span
        ]
    ).astype(BF16)
    feed_shard = lax.psum_scatter(grad_feed, "dp", scatter_dimension=1, tiled=True)
    grad_down = total_of([dot_rows(hidden[k], feed_grad[k]) for k in span]).astype(BF16)
    down_shard = lax.psum_scatter(grad_down, "dp", scatter_dimension=1, tiled=True)

    c_grad, conv_grad = [], []
    for k in span:
        rows_grad = dot_last(mixer_grad[k], weight_out)
        c_grad.append(rows_grad * conv[k])
        conv_grad.append(rows_grad * gates[k][1])
    grad_out_weight = total_of([dot_rows(mixer_rows[k], mixer_grad[k]) for k in span])
    out_shard = lax.psum_scatter(
        grad_out_weight.astype(BF16), "dp", scatter_dimension=1, tiled=True
    )
    grad_taps = jnp.stack(
        [
            total_of([jnp.sum(conv_grad[k] * prev_two[k], axis=0) for k in span]),
            total_of([jnp.sum(conv_grad[k] * prev_one[k], axis=0) for k in span]),
            total_of([jnp.sum(conv_grad[k] * mixed[k], axis=0) for k in span]),
        ]
    )
    gates_grad, gain_one_parts, tokens_grad = [], [], []
    for k in span:
        edge = jnp.zeros((2, part_width), F32)
        last = k == CHUNKS - 1
        after_one = edge if last else conv_grad[k + 1][:2] * same_one[k + 1][:2]
        after_two = edge if last else conv_grad[k + 1][:2] * same_two[k + 1][:2]
        next_one = jnp.concatenate([(conv_grad[k] * same_one[k])[1:], after_one[:1]], axis=0)
        next_two = jnp.concatenate([(conv_grad[k] * same_two[k])[2:], after_two], axis=0)
        mixed_grad = taps[2] * conv_grad[k] + taps[1] * next_one + taps[0] * next_two
        b_grad, x_grad = mixed_grad * gates[k][2], mixed_grad * gates[k][0]
        inner = sum_tensor(
            jnp.sum(b_grad * gates[k][0] + c_grad[k] * gates[k][1] + x_grad * gates[k][2], axis=1)
        )
        gates_grad.append(jnp.stack([b_grad, c_grad[k], x_grad]).astype(BF16))
        normed_grad = scatter_columns(
            jnp.einsum("gte,gde->td", gates_grad[k], in_sent, preferred_element_type=F32),
            jnp.einsum("gte,gde->td", gates_grad[k], in_kept, preferred_element_type=F32),
        )
        unit = token_parts[k].astype(F32) * scale_one[k]
        gain_one_parts.append(jnp.sum(normed_grad * unit, axis=0))
        tokens_grad.append(
            middle_grad[k]
            + scale_one[k]
            * (normed_grad * gain_one.astype(F32) - unit * (inner / full_width)[:, None])
        )
    grad_in_weight = total_of(
        [
            jnp.einsum("td,gte->gde", normed_one[k], gates_grad[k], preferred_element_type=F32)
            for k in span
        ]
    ).astype(BF16)
    in_shard = lax.psum_scatter(grad_in_weight, "dp", scatter_dimension=1, tiled=True)

    for k in span:
        feed_out = scatter_columns(
            jnp.dot(hidden[k], down_sent, preferred_element_type=F32),
            jnp.dot(hidden[k], down_kept, preferred_element_type=F32),
        )
        block_out.append((middle[k] + live[k] * feed_out).astype(BF16))

    small = sum_groups(jnp.concatenate([total_of(gain_two_parts)[None], grad_taps], axis=0))
    gain_one_sum = sum_groups(total_of(gain_one_parts))
    return (
        jnp.concatenate(block_out, axis=0),
        jnp.concatenate([part.astype(BF16) for part in tokens_grad], axis=0),
        gain_one_sum,
        in_shard.astype(F32),
        small[1:],
        out_shard.astype(F32),
        small[0],
        feed_shard.astype(F32),
        down_shard.astype(F32),
    )


def solution(mesh):
    placed = (
        P("dp", "tensor"),
        P("dp", None),
        P("tensor"),
        P(None, None, "tensor"),
        P(None, "tensor"),
        P("tensor", None),
        P("tensor"),
        P(None, None, "tensor"),
        P("tensor", None),
        P("dp", "tensor"),
    )
    return jax.shard_map(
        body,
        mesh=mesh,
        in_specs=placed,
        out_specs=(
            P("dp", "tensor"),
            P("dp", "tensor"),
            P("tensor"),
            P(None, "dp", "tensor"),
            P(None, "tensor"),
            P("tensor", "dp"),
            P("tensor"),
            P(None, "dp", "tensor"),
            P("tensor", "dp"),
        ),
        check_vma=False,
    )
```

```python
import jax
import jax.numpy as jnp
from jax import lax
from jax.sharding import PartitionSpec as P

EPSILON = 1e-05
CHUNKS = 2
F32 = jnp.float32
BF16 = jnp.bfloat16


def swap_core(values):
    size = lax.axis_size("tensor")
    return lax.ppermute(values, "tensor", [(i, i ^ 1) for i in range(size)])


def swap_chip(values):
    size = lax.axis_size("tensor")
    return lax.ppermute(values, "tensor", [(i, i ^ 2) for i in range(size)])


def ordered(is_first, own, other):
    return jnp.where(
        is_first,
        jnp.concatenate([own, other], axis=-1),
        jnp.concatenate([other, own], axis=-1),
    )


def gather_columns(values, core, chip):
    from_chip = swap_chip(values)
    from_core = swap_core(values)
    from_both = swap_core(from_chip)
    near = ordered(core == 0, values, from_core)
    far = ordered(core == 0, from_chip, from_both)
    return ordered(chip == 0, near, far)


def split_columns(weight, axis, core, chip):
    width = weight.shape[axis] // 4

    def block(chip_at, core_at):
        return lax.dynamic_slice_in_dim(weight, (chip_at * 2 + core_at) * width, width, axis)

    kept = jnp.concatenate([block(1 - chip, core), block(chip, core)], axis=axis)
    sent = jnp.concatenate([block(1 - chip, 1 - core), block(chip, 1 - core)], axis=axis)
    return sent, kept


def after(values, *others):
    return lax.optimization_barrier((values,) + others)[0]


def scatter_all(pairs, *others):
    kept_last = tuple(kept for sent, kept in pairs)
    results = []
    for k, (sent, kept) in enumerate(pairs):
        total = kept + swap_core(sent).astype(F32)
        width = total.shape[1] // 2
        received = swap_chip(total[:, :width].astype(BF16))
        received = after(received, *kept_last[k + 1 :], *others)
        results.append(total[:, width:] + received.astype(F32))
    return results


def sum_tensor(values):
    values = values + swap_core(values)
    return values + swap_chip(values)


def sum_groups(values):
    size = lax.axis_size("dp")
    step = 1
    while step < size:
        values = values + lax.ppermute(values, "dp", [(i, i ^ step) for i in range(size)])
        step *= 2
    return values


def scatter_groups(values):
    size = lax.axis_size("dp")
    index = lax.axis_index("dp")
    block = values.shape[0] // size
    step = 1
    while step < size:
        pairs = values.reshape(-1, 2, block, values.shape[-1])
        bit = (index // step) % 2
        sent = lax.dynamic_index_in_dim(pairs, 1 - bit, 1, keepdims=False).astype(BF16)
        kept = lax.dynamic_index_in_dim(pairs, bit, 1, keepdims=False)
        moved = lax.ppermute(sent, "dp", [(i, i ^ step) for i in range(size)])
        values = kept + moved.astype(F32)
        step *= 2
    return values.reshape(block, -1)


def total_of(parts):
    result = parts[0]
    for part in parts[1:]:
        result = result + part
    return result


def dot_rows(left, right):
    return lax.dot_general(left, right, (((0,), (0,)), ((), ())), preferred_element_type=F32)


def dot_last(left, right):
    return lax.dot_general(left, right, (((1,), (1,)), ((), ())), preferred_element_type=F32)


def body(
    tokens,
    lengths,
    gain_one,
    weight_in,
    conv_taps,
    weight_out,
    gain_two,
    weight_feed,
    weight_down,
    grad_out,
):
    row_count = tokens.shape[0]
    part_width = tokens.shape[1]
    full_width = part_width * lax.axis_size("tensor")
    index = lax.axis_index("tensor")
    core, chip = index % 2, index // 2
    doc_ends = jnp.cumsum(lengths[0])
    positions = jnp.arange(row_count, dtype=jnp.int32)
    segments = jnp.sum((positions[:, None] >= doc_ends[None, :]).astype(jnp.int32), axis=1)
    live_all = (positions < doc_ends[-1]).astype(F32)[:, None]
    same_one_all = jnp.concatenate(
        [jnp.zeros((1,), F32), (segments[1:] == segments[:-1]).astype(F32)]
    )[:, None]
    same_two_all = jnp.concatenate(
        [jnp.zeros((2,), F32), (segments[2:] == segments[:-2]).astype(F32)]
    )[:, None]
    rows = row_count // CHUNKS

    def cut(array):
        return [array[k * rows : (k + 1) * rows] for k in range(CHUNKS)]

    live, same_one, same_two = cut(live_all), cut(same_one_all), cut(same_two_all)
    token_parts, grad_parts = cut(tokens), cut(grad_out)
    span = range(CHUNKS)

    gains = gather_columns(jnp.stack([gain_one, gain_two]), core, chip).astype(F32)
    gain_one_full, gain_two_full = gains[0:1], gains[1:2]
    token_full = [gather_columns(part, core, chip) for part in token_parts]
    held = lax.optimization_barrier(tuple(grad_parts) + tuple(token_full))
    grad_later, token_full = held[:CHUNKS], held[CHUNKS:]

    out_sent, out_kept = split_columns(weight_out, 1, core, chip)
    down_sent, down_kept = split_columns(weight_down, 1, core, chip)
    feed_sent, feed_kept = split_columns(weight_feed, 1, core, chip)
    in_sent, in_kept = split_columns(weight_in, 1, core, chip)
    taps = conv_taps.astype(F32)

    normed_one, gates, mixed, prev_one, prev_two, conv = [], [], [], [], [], []
    mixer_rows, mixer_parts, middle, middle_full, scale_one = [], [], [], [], []
    for k in span:
        wide = token_full[k].astype(F32)
        scale = lax.rsqrt(jnp.mean(wide * wide, axis=1, keepdims=True) + EPSILON)
        scale_one.append(scale)
        normed_one.append((wide * scale * gain_one_full).astype(BF16))
        gate = jnp.einsum("td,gde->gte", normed_one[k], weight_in, preferred_element_type=F32)
        gates.append(gate)
        mix = gate[0] * gate[2]
        mixed.append(mix)
        before = mixed[k - 1][-2:] if k else jnp.zeros((2, part_width), F32)
        extended = jnp.concatenate([before, mix], axis=0)
        prev_one.append(extended[1:-1] * same_one[k])
        prev_two.append(extended[:-2] * same_two[k])
        conv.append(taps[2] * mix + taps[1] * prev_one[k] + taps[0] * prev_two[k])
        mixer_rows.append((gate[1] * conv[k]).astype(BF16))
        mixer_parts.append(
            (
                jnp.dot(mixer_rows[k], out_sent, preferred_element_type=F32).astype(BF16),
                jnp.dot(mixer_rows[k], out_kept, preferred_element_type=F32),
            )
        )
    for k, mixer_out in enumerate(scatter_all(mixer_parts)):
        middle.append(token_parts[k].astype(F32) + live[k] * mixer_out)
        middle_full.append(gather_columns(middle[k].astype(BF16), core, chip))

    grad_full = [gather_columns(part, core, chip) for part in grad_later]
    normed_two, hidden, feed_grad, gu_grad, block_out = [], [], [], [], []
    middle_grad, mixer_grad, gain_two_parts = [], [], []
    scale_two, inner_two, feed_parts = [], [], []
    for k in span:
        wide = middle_full[k].astype(F32)
        scale = lax.rsqrt(jnp.mean(wide * wide, axis=1, keepdims=True) + EPSILON)
        normed_two.append((wide * scale * gain_two_full).astype(BF16))
        gate_up = jnp.einsum("td,kdf->ktf", normed_two[k], weight_feed, preferred_element_type=F32)
        gate, up = gate_up[0], gate_up[1]
        sigmoid = jax.nn.sigmoid(gate)
        hidden.append((gate * sigmoid * up).astype(BF16))
        feed_grad.append(jnp.where(live[k] > 0.0, grad_full[k], jnp.zeros_like(grad_full[k])))
        hidden_grad = dot_last(feed_grad[k], weight_down)
        gate_grad = hidden_grad * up * sigmoid * (1.0 + gate * (1.0 - sigmoid))
        up_grad = hidden_grad * (gate * sigmoid)
        scale_two.append(scale)
        inner_two.append(sum_tensor(jnp.sum(gate_grad * gate + up_grad * up, axis=1)))
        gu_grad.append(jnp.stack([gate_grad, up_grad]).astype(BF16))
        feed_parts.append(
            (
                jnp.einsum(
                    "ktf,kdf->td", gu_grad[k], feed_sent, preferred_element_type=F32
                ).astype(BF16),
                jnp.einsum("ktf,kdf->td", gu_grad[k], feed_kept, preferred_element_type=F32),
            )
        )
    grad_down = total_of([dot_rows(feed_grad[k], hidden[k]) for k in span])
    for k, normed_grad in enumerate(scatter_all(feed_parts)):
        scale, inner = scale_two[k], inner_two[k]
        unit = middle[k] * scale
        gain_two_parts.append(jnp.sum(normed_grad * unit, axis=0))
        middle_grad.append(
            grad_parts[k].astype(F32)
            + scale
            * (normed_grad * gain_two.astype(F32) - unit * (inner / full_width)[:, None])
        )
        mixer_grad.append(gather_columns((middle_grad[k] * live[k]).astype(BF16), core, chip))
    grad_feed = [
        total_of([dot_rows(normed_two[k], gu_grad[k][side]) for k in span]) for side in range(2)
    ]
    down_parts = [
        (
            jnp.dot(hidden[k], down_sent, preferred_element_type=F32).astype(BF16),
            jnp.dot(hidden[k], down_kept, preferred_element_type=F32),
        )
        for k in span
    ]
    down_shard = scatter_groups(grad_down)
    feed_shard = [scatter_groups(part) for part in grad_feed]
    mixer_grad = [after(mixer_grad[0], grad_down)] + [
        after(part, *grad_feed, *[kept for sent, kept in down_parts]) for part in mixer_grad[1:]
    ]

    c_grad, conv_grad = [], []
    for k in span:
        rows_grad = dot_last(mixer_grad[k], weight_out)
        c_grad.append(rows_grad * conv[k])
        conv_grad.append(rows_grad * gates[k][1])
    out_shard = scatter_groups(
        total_of([dot_rows(mixer_grad[k], mixer_rows[k]) for k in span])
    )
    grad_taps = jnp.stack(
        [
            total_of([jnp.sum(conv_grad[k] * prev_two[k], axis=0) for k in span]),
            total_of([jnp.sum(conv_grad[k] * prev_one[k], axis=0) for k in span]),
            total_of([jnp.sum(conv_grad[k] * mixed[k], axis=0) for k in span]),
        ]
    )
    gates_grad, gain_one_parts, tokens_grad = [], [], []
    inner_one, in_parts = [], []
    for k in span:
        edge = jnp.zeros((2, part_width), F32)
        last = k == CHUNKS - 1
        after_one = edge if last else conv_grad[k + 1][:2] * same_one[k + 1][:2]
        after_two = edge if last else conv_grad[k + 1][:2] * same_two[k + 1][:2]
        next_one = jnp.concatenate([(conv_grad[k] * same_one[k])[1:], after_one[:1]], axis=0)
        next_two = jnp.concatenate([(conv_grad[k] * same_two[k])[2:], after_two], axis=0)
        mixed_grad = taps[2] * conv_grad[k] + taps[1] * next_one + taps[0] * next_two
        b_grad, x_grad = mixed_grad * gates[k][2], mixed_grad * gates[k][0]
        inner_one.append(
            sum_tensor(
                jnp.sum(
                    b_grad * gates[k][0] + c_grad[k] * gates[k][1] + x_grad * gates[k][2], axis=1
                )
            )
        )
        gates_grad.append(jnp.stack([b_grad, c_grad[k], x_grad]).astype(BF16))
        in_parts.append(
            (
                jnp.einsum(
                    "gte,gde->td", gates_grad[k], in_sent, preferred_element_type=F32
                ).astype(BF16),
                jnp.einsum("gte,gde->td", gates_grad[k], in_kept, preferred_element_type=F32),
            )
        )
    grad_in = [
        total_of([dot_rows(normed_one[k], gates_grad[k][side]) for k in span]) for side in range(3)
    ]
    in_shard = scatter_groups(jnp.concatenate(grad_in, axis=1))
    for k, normed_grad in enumerate(scatter_all(in_parts, *grad_in)):
        unit = token_parts[k].astype(F32) * scale_one[k]
        gain_one_parts.append(jnp.sum(normed_grad * unit, axis=0))
        tokens_grad.append(
            middle_grad[k]
            + scale_one[k]
            * (normed_grad * gain_one.astype(F32) - unit * (inner_one[k] / full_width)[:, None])
        )

    for k, feed_out in enumerate(scatter_all(down_parts)):
        block_out.append((middle[k] + live[k] * feed_out).astype(BF16))

    small = sum_groups(jnp.concatenate([total_of(gain_two_parts)[None], grad_taps], axis=0))
    gain_one_sum = sum_groups(total_of(gain_one_parts))
    return (
        jnp.concatenate(block_out, axis=0),
        jnp.concatenate([part.astype(BF16) for part in tokens_grad], axis=0),
        gain_one_sum,
        jnp.stack(jnp.split(in_shard, 3, axis=1)),
        small[1:],
        out_shard.T,
        small[0],
        jnp.stack(feed_shard),
        down_shard.T,
    )


def solution(mesh):
    placed = (
        P("dp", "tensor"),
        P("dp", None),
        P("tensor"),
        P(None, None, "tensor"),
        P(None, "tensor"),
        P("tensor", None),
        P("tensor"),
        P(None, None, "tensor"),
        P("tensor", None),
        P("dp", "tensor"),
    )
    return jax.shard_map(
        body,
        mesh=mesh,
        in_specs=placed,
        out_specs=(
            P("dp", "tensor"),
            P("dp", "tensor"),
            P("tensor"),
            P(None, "dp", "tensor"),
            P(None, "tensor"),
            P("tensor", "dp"),
            P("tensor"),
            P(None, "dp", "tensor"),
            P("tensor", "dp"),
        ),
        check_vma=False,
    )
```

```python
import jax
import jax.numpy as jnp
from jax import lax
from jax.sharding import PartitionSpec as P

EPSILON = 1e-05
CHUNKS = 2
F32 = jnp.float32
BF16 = jnp.bfloat16


def swap_core(values):
    size = lax.axis_size("tensor")
    return lax.ppermute(values, "tensor", [(i, i ^ 1) for i in range(size)])


def swap_chip(values):
    size = lax.axis_size("tensor")
    return lax.ppermute(values, "tensor", [(i, i ^ 2) for i in range(size)])


def ordered(is_first, own, other):
    return jnp.where(
        is_first,
        jnp.concatenate([own, other], axis=-1),
        jnp.concatenate([other, own], axis=-1),
    )


def gather_columns(values, core, chip, *others, fetched=None):
    from_chip = swap_chip(values) if fetched is None else fetched
    if others:
        from_chip = after(from_chip, *others)
    from_core = swap_core(values)
    from_both = swap_core(from_chip)
    near = ordered(core == 0, values, from_core)
    far = ordered(core == 0, from_chip, from_both)
    return ordered(chip == 0, near, far)


def split_columns(weight, axis, core, chip):
    width = weight.shape[axis] // 4

    def block(chip_at, core_at):
        return lax.dynamic_slice_in_dim(weight, (chip_at * 2 + core_at) * width, width, axis)

    kept = jnp.concatenate([block(1 - chip, core), block(chip, core)], axis=axis)
    sent = jnp.concatenate([block(1 - chip, 1 - core), block(chip, 1 - core)], axis=axis)
    return sent, kept


def after(values, *others):
    return lax.optimization_barrier((values,) + others)[0]


def scatter_all(pairs, *others):
    kept_last = tuple(kept for sent, kept in pairs)
    results = []
    for k, (sent, kept) in enumerate(pairs):
        total = kept + swap_core(sent).astype(F32)
        width = total.shape[1] // 2
        received = swap_chip(total[:, :width].astype(BF16))
        received = after(received, *kept_last[k + 1 :], *others)
        results.append(total[:, width:] + received.astype(F32))
    return results


def sum_tensor(values):
    values = values + swap_core(values)
    return values + swap_chip(values)


def sum_groups(values):
    size = lax.axis_size("dp")
    step = 1
    while step < size:
        values = values + lax.ppermute(values, "dp", [(i, i ^ step) for i in range(size)])
        step *= 2
    return values


def scatter_groups(values, swapped=False, holds=()):
    size = lax.axis_size("dp")
    index = lax.axis_index("dp")
    block = values.shape[0] // size
    left = [step for step in (1 << bit for bit in range(size.bit_length() - 1))]
    order = list(left)
    if swapped:
        order[:2] = order[:2][::-1]
    for place, step in enumerate(order):
        lower = 1 << left.index(step)
        left.remove(step)
        pairs = values.reshape(-1, 2, lower * block, values.shape[-1])
        bit = (index // step) % 2
        sent = lax.dynamic_index_in_dim(pairs, 1 - bit, 1, keepdims=False).astype(BF16)
        kept = lax.dynamic_index_in_dim(pairs, bit, 1, keepdims=False)
        moved = lax.ppermute(sent, "dp", [(i, i ^ step) for i in range(size)])
        if place < len(holds):
            moved = after(moved, *holds[place])
        values = kept + moved.astype(F32)
    return values.reshape(block, -1)


def total_of(parts):
    result = parts[0]
    for part in parts[1:]:
        result = result + part
    return result


def dot_rows(left, right):
    return lax.dot_general(left, right, (((0,), (0,)), ((), ())), preferred_element_type=F32)


def dot_last(left, right):
    return lax.dot_general(left, right, (((1,), (1,)), ((), ())), preferred_element_type=F32)


def body(
    tokens,
    lengths,
    gain_one,
    weight_in,
    conv_taps,
    weight_out,
    gain_two,
    weight_feed,
    weight_down,
    grad_out,
):
    row_count = tokens.shape[0]
    part_width = tokens.shape[1]
    full_width = part_width * lax.axis_size("tensor")
    index = lax.axis_index("tensor")
    core, chip = index % 2, index // 2
    doc_ends = jnp.cumsum(lengths[0])
    positions = jnp.arange(row_count, dtype=jnp.int32)
    segments = jnp.sum((positions[:, None] >= doc_ends[None, :]).astype(jnp.int32), axis=1)
    live_all = (positions < doc_ends[-1]).astype(F32)[:, None]
    same_one_all = jnp.concatenate(
        [jnp.zeros((1,), F32), (segments[1:] == segments[:-1]).astype(F32)]
    )[:, None]
    same_two_all = jnp.concatenate(
        [jnp.zeros((2,), F32), (segments[2:] == segments[:-2]).astype(F32)]
    )[:, None]
    rows = row_count // CHUNKS

    def cut(array):
        return [array[k * rows : (k + 1) * rows] for k in range(CHUNKS)]

    live, same_one, same_two = cut(live_all), cut(same_one_all), cut(same_two_all)
    token_parts, grad_parts = cut(tokens), cut(grad_out)
    span = range(CHUNKS)

    gains = gather_columns(jnp.stack([gain_one, gain_two]), core, chip).astype(F32)
    gain_one_full, gain_two_full = gains[0:1], gains[1:2]
    token_far = [swap_chip(part) for part in token_parts]
    token_full = [
        gather_columns(part, core, chip, fetched=far) for part, far in zip(token_parts, token_far)
    ]
    grad_far = [swap_chip(after(part, far)) for part, far in zip(grad_parts, token_far)]

    out_sent, out_kept = split_columns(weight_out, 1, core, chip)
    down_sent, down_kept = split_columns(weight_down, 1, core, chip)
    feed_sent, feed_kept = split_columns(weight_feed, 1, core, chip)
    in_sent, in_kept = split_columns(weight_in, 1, core, chip)
    taps = conv_taps.astype(F32)

    normed_one, gates, mixed, prev_one, prev_two, conv = [], [], [], [], [], []
    mixer_rows, mixer_parts, middle, middle_full, scale_one = [], [], [], [], []
    for k in span:
        wide = token_full[k].astype(F32)
        scale = lax.rsqrt(jnp.mean(wide * wide, axis=1, keepdims=True) + EPSILON)
        scale_one.append(scale)
        normed_one.append((wide * scale * gain_one_full).astype(BF16))
        gate = jnp.einsum("td,gde->gte", normed_one[k], weight_in, preferred_element_type=F32)
        gates.append(gate)
        mix = gate[0] * gate[2]
        mixed.append(mix)
        before = mixed[k - 1][-2:] if k else jnp.zeros((2, part_width), F32)
        extended = jnp.concatenate([before, mix], axis=0)
        prev_one.append(extended[1:-1] * same_one[k])
        prev_two.append(extended[:-2] * same_two[k])
        conv.append(taps[2] * mix + taps[1] * prev_one[k] + taps[0] * prev_two[k])
        mixer_rows.append((gate[1] * conv[k]).astype(BF16))
        mixer_parts.append(
            (
                jnp.dot(mixer_rows[k], out_sent, preferred_element_type=F32).astype(BF16),
                jnp.dot(mixer_rows[k], out_kept, preferred_element_type=F32),
            )
        )
    mixer_parts = [(sent, after(kept, *grad_far)) for sent, kept in mixer_parts]
    for k, mixer_out in enumerate(scatter_all(mixer_parts)):
        middle.append(token_parts[k].astype(F32) + live[k] * mixer_out)

    grad_full = [
        gather_columns(part, core, chip, fetched=far) for part, far in zip(grad_parts, grad_far)
    ]
    normed_two, hidden, feed_grad, gu_grad, block_out = [], [], [], [], []
    middle_grad, mixer_grad, gain_two_parts = [], [], []
    scale_two, inner_two, feed_parts = [], [], []
    for k in span:
        earlier = [kept for sent, kept in feed_parts]
        middle_full.append(gather_columns(middle[k].astype(BF16), core, chip, *earlier))
        wide = middle_full[k].astype(F32)
        scale = lax.rsqrt(jnp.mean(wide * wide, axis=1, keepdims=True) + EPSILON)
        normed_two.append((wide * scale * gain_two_full).astype(BF16))
        gate_up = jnp.einsum("td,kdf->ktf", normed_two[k], weight_feed, preferred_element_type=F32)
        gate, up = gate_up[0], gate_up[1]
        sigmoid = jax.nn.sigmoid(gate)
        hidden.append((gate * sigmoid * up).astype(BF16))
        feed_grad.append(jnp.where(live[k] > 0.0, grad_full[k], jnp.zeros_like(grad_full[k])))
        hidden_grad = dot_last(feed_grad[k], weight_down)
        gate_grad = hidden_grad * up * sigmoid * (1.0 + gate * (1.0 - sigmoid))
        up_grad = hidden_grad * (gate * sigmoid)
        scale_two.append(scale)
        inner_two.append(sum_tensor(jnp.sum(gate_grad * gate + up_grad * up, axis=1)))
        gu_grad.append(jnp.stack([gate_grad, up_grad]).astype(BF16))
        feed_parts.append(
            (
                jnp.einsum(
                    "ktf,kdf->td", gu_grad[k], feed_sent, preferred_element_type=F32
                ).astype(BF16),
                jnp.einsum("ktf,kdf->td", gu_grad[k], feed_kept, preferred_element_type=F32),
            )
        )
    grad_down = total_of([dot_rows(feed_grad[k], hidden[k]) for k in span])
    for k, normed_grad in enumerate(scatter_all(feed_parts)):
        scale, inner = scale_two[k], inner_two[k]
        unit = middle[k] * scale
        gain_two_parts.append(jnp.sum(normed_grad * unit, axis=0))
        middle_grad.append(
            grad_parts[k].astype(F32)
            + scale
            * (normed_grad * gain_two.astype(F32) - unit * (inner / full_width)[:, None])
        )
        mixer_grad.append(gather_columns((middle_grad[k] * live[k]).astype(BF16), core, chip))
    grad_feed = [
        total_of([dot_rows(normed_two[k], gu_grad[k][side]) for k in span]) for side in range(2)
    ]
    down_parts = [
        (
            jnp.dot(hidden[k], down_sent, preferred_element_type=F32).astype(BF16),
            jnp.dot(hidden[k], down_kept, preferred_element_type=F32),
        )
        for k in span
    ]
    mixer_grad = [after(mixer_grad[0], grad_down)] + [
        after(part, *grad_feed, *[kept for sent, kept in down_parts]) for part in mixer_grad[1:]
    ]

    c_grad, conv_grad = [], []
    for k in span:
        rows_grad = dot_last(mixer_grad[k], weight_out)
        c_grad.append(rows_grad * conv[k])
        conv_grad.append(rows_grad * gates[k][1])
    out_shard = scatter_groups(
        total_of([dot_rows(mixer_grad[k], mixer_rows[k]) for k in span])
    )
    grad_taps = jnp.stack(
        [
            total_of([jnp.sum(conv_grad[k] * prev_two[k], axis=0) for k in span]),
            total_of([jnp.sum(conv_grad[k] * prev_one[k], axis=0) for k in span]),
            total_of([jnp.sum(conv_grad[k] * mixed[k], axis=0) for k in span]),
        ]
    )
    gates_grad, gain_one_parts, tokens_grad = [], [], []
    inner_one, in_parts = [], []
    for k in span:
        edge = jnp.zeros((2, part_width), F32)
        last = k == CHUNKS - 1
        after_one = edge if last else conv_grad[k + 1][:2] * same_one[k + 1][:2]
        after_two = edge if last else conv_grad[k + 1][:2] * same_two[k + 1][:2]
        next_one = jnp.concatenate([(conv_grad[k] * same_one[k])[1:], after_one[:1]], axis=0)
        next_two = jnp.concatenate([(conv_grad[k] * same_two[k])[2:], after_two], axis=0)
        mixed_grad = taps[2] * conv_grad[k] + taps[1] * next_one + taps[0] * next_two
        b_grad, x_grad = mixed_grad * gates[k][2], mixed_grad * gates[k][0]
        inner_one.append(
            sum_tensor(
                jnp.sum(
                    b_grad * gates[k][0] + c_grad[k] * gates[k][1] + x_grad * gates[k][2], axis=1
                )
            )
        )
        gates_grad.append(jnp.stack([b_grad, c_grad[k], x_grad]).astype(BF16))
        in_parts.append(
            (
                jnp.einsum(
                    "gte,gde->td", gates_grad[k], in_sent, preferred_element_type=F32
                ).astype(BF16),
                jnp.einsum("gte,gde->td", gates_grad[k], in_kept, preferred_element_type=F32),
            )
        )
    grad_in = [
        total_of([dot_rows(normed_one[k], gates_grad[k][side]) for k in span]) for side in range(3)
    ]
    in_shard = scatter_groups(jnp.concatenate(grad_in, axis=1))
    holds = ((conv_grad[0],), (gates_grad[0],))
    down_shard = scatter_groups(grad_down, False, holds)
    feed_shard = [
        scatter_groups(part, swapped, holds) for part, swapped in zip(grad_feed, (True, False))
    ]
    for k, normed_grad in enumerate(scatter_all(in_parts, *grad_in)):
        unit = token_parts[k].astype(F32) * scale_one[k]
        gain_one_parts.append(jnp.sum(normed_grad * unit, axis=0))
        tokens_grad.append(
            middle_grad[k]
            + scale_one[k]
            * (normed_grad * gain_one.astype(F32) - unit * (inner_one[k] / full_width)[:, None])
        )

    for k, feed_out in enumerate(scatter_all(down_parts)):
        block_out.append((middle[k] + live[k] * feed_out).astype(BF16))

    small = sum_groups(jnp.concatenate([total_of(gain_two_parts)[None], grad_taps], axis=0))
    gain_one_sum = sum_groups(total_of(gain_one_parts))
    return (
        jnp.concatenate(block_out, axis=0),
        jnp.concatenate([part.astype(BF16) for part in tokens_grad], axis=0),
        gain_one_sum,
        jnp.stack(jnp.split(in_shard, 3, axis=1)),
        small[1:],
        out_shard.T,
        small[0],
        jnp.stack(feed_shard),
        down_shard.T,
    )


def solution(mesh):
    placed = (
        P("dp", "tensor"),
        P("dp", None),
        P("tensor"),
        P(None, None, "tensor"),
        P(None, "tensor"),
        P("tensor", None),
        P("tensor"),
        P(None, None, "tensor"),
        P("tensor", None),
        P("dp", "tensor"),
    )
    return jax.shard_map(
        body,
        mesh=mesh,
        in_specs=placed,
        out_specs=(
            P("dp", "tensor"),
            P("dp", "tensor"),
            P("tensor"),
            P(None, "dp", "tensor"),
            P(None, "tensor"),
            P("tensor", "dp"),
            P("tensor"),
            P(None, "dp", "tensor"),
            P("tensor", "dp"),
        ),
        check_vma=False,
    )
```
